512 devices in a mesh: grp: 16 (over z), seq: 32 (over x, y, core).
Axes of the slice: x: 4, y: 4, z: 16, core: 2. Of those that a mesh axis runs over, the one named last changes fastest.
Arguments:
- queries: bfloat16 [1024, 4096], P('grp', 'seq'), may hold values from -30 to 30
- row_prompt: int32 [1024, 1], P('grp'), may hold values from 0 to 15; in each aligned block of 64 rows (0 to 63, 64 to 127, ...) at most 8 rows name the same one
- prompt_prefix_keys: bfloat16 [16, 32768, 512], P('grp', 'seq'), may hold values from -30 to 30
- prompt_prefix_values: bfloat16 [16, 32768, 512], P('grp', 'seq'), may hold values from -6 to 6
- row_suffix_keys: bfloat16 [1024, 128, 512], P(('grp', 'seq')), may hold values from -12 to 12
- row_suffix_values: bfloat16 [1024, 128, 512], P(('grp', 'seq')), may hold values from -6 to 6
- suffix_lengths: int32 [1024], P(('grp', 'seq')), may hold values from 1 to 128, as said below
- w_out: bfloat16 [4096, 8192], P('seq'), may hold values from -0.75 to 0.75
Outputs:
- mixed: bfloat16 [1024, 8192], P('grp', 'seq')
The draws below stay inside these ranges and needn't reach their ends.
Inputs may be any that keep to these rules, and one draw needn't show every extreme that they name: `row_prompt`: among the 64 rows of one group no prompt is named by more than 8 rows, and some prompt reaches 8 in some groups; every prompt is named by some row. `suffix_lengths`: every draw holds a row with 128 live positions.
All inputs are finite; a program needn't handle non-finite values.
Results may differ from the reference program's by a relative error of at most 0.022.
Values may be sent and summed in bfloat16 or wider, within the bound.
No kernel may reach another device: no remote copies, remote signals or barrier semaphores. Data moves between devices by JAX's collectives and lax.ppermute only.
A program may use at most 128 MiB of HBM per device.

```python
import math
import jax
import jax.numpy as jnp
import numpy as np
from jax import lax

D = 8192
QUERY_HEADS = 32
KEY_VALUE_HEADS = 4
HEAD_SIZE = 128
SUFFIX_SLOTS = 128
ROW_GRP = 64
PROMPTS = 16
PREFIX = 32768
ROWS = 1024
CAP = 8
QUERY_WIDTH = 4096
KVW = 512


def draw_queries(key, part):
    key = jax.random.fold_in(key, 11)
    first = jax.random.fold_in(key, 0)
    base = jax.random.normal(first, (ROWS, QUERY_WIDTH), dtype=jnp.float32)
    return jnp.clip(base, -30.0, 30.0).astype(jnp.bfloat16)


def draw_prompt_prefix_keys(key, part):
    key = jax.random.fold_in(key, 12)
    first = jax.random.fold_in(key, 0)
    place = jnp.arange(PREFIX, dtype=jnp.int32)
    rising = 1.2 + place.astype(jnp.float32) / PREFIX
    base = jax.random.normal(first, (PROMPTS, PREFIX, KVW), dtype=jnp.float32) * rising[None, :, None]
    return jnp.clip(base, -30.0, 30.0).astype(jnp.bfloat16)


def draw_suffix_lengths(key, part):
    key = jax.random.fold_in(key, 13)
    first, second = jax.random.split(key)
    whole = jax.random.randint(first, (ROWS,), 0, 4) == 0
    lengths = jax.random.randint(second, (ROWS,), 1, SUFFIX_SLOTS + 1)
    lengths = jnp.where(whole, SUFFIX_SLOTS, lengths)
    lengths = jnp.where(jnp.arange(ROWS, dtype=jnp.int32) == 0, SUFFIX_SLOTS, lengths)
    return lengths.astype(jnp.int32)


def with_spikes(result, stream_key, source, target, blocks, factor):
    def block_of(dim):
        return (jnp.arange(result.shape[dim]) // (result.shape[dim] // blocks)).reshape((-1,) + (1,) * (result.ndim - 1 - dim))

    near = jax.random.permutation(stream_key, blocks)[block_of(target)]
    second = (block_of(target) + blocks // 2) % blocks
    return jnp.where((block_of(source) == near) | (block_of(source) == second), factor * result, result)


def block_levels(stream_key, shape, cuts, smallest, top_value):
    gain, own = 1.0, jax.random.fold_in(stream_key, 6)
    for dim, parts in cuts:
        steps = jnp.exp(jax.random.uniform(jax.random.fold_in(own, dim), (parts,), jnp.float32, smallest / len(cuts), top_value / len(cuts)))
        gain = gain * jnp.repeat(steps, shape[dim] // parts).reshape([-1 if axis == dim else 1 for axis in range(len(shape))])
    return gain


def deal_out(own_key, own, number, rows, count, top, bound, lean):
    order = jax.random.permutation(own_key, count)
    crowded, common = load_shares(count, rows * top, bound, lean, True), load_shares(count, rows * top, bound, lean, False)
    places = jnp.arange(count)

    def named(sizes, rotation):
        used = int((sizes > 0).sum())
        fixed = max(1, used // 4)
        passed = fixed + (places - fixed + rotation * (used - fixed)) % max(1, count - fixed)
        return jnp.zeros((count,), jnp.int32).at[order[jnp.where(places < fixed, places, passed)]].set(jnp.asarray(sizes, jnp.int32))

    sizes = jnp.where(number % 4 == 0, named(crowded, number // 4), named(common, number - number // 4 - 1))
    mixed = jax.random.permutation(jax.random.fold_in(own, 3), count)
    giver, receiver = mixed[0:count // 2 * 2:2], mixed[1:count // 2 * 2:2]
    slack = jnp.minimum(sizes[giver] - 1, bound - sizes[receiver]) // 2
    slack = jnp.where((giver == order[0]) | (receiver == order[0]) | (sizes[receiver] == 0), 0, jnp.maximum(slack, 0))
    passed = jax.random.randint(jax.random.fold_in(own, 4), (count // 2,), 0, 1 << 20) % (slack + 1)
    sizes = sizes.at[giver].add(-passed).at[receiver].add(passed)
    members = jnp.searchsorted(jnp.cumsum(sizes), jnp.arange(rows * top), side="right").astype(jnp.int32)
    grid = members.reshape(top, rows).T
    grid = grid[jax.random.permutation(jax.random.fold_in(own, 1), rows)]
    rotation = jax.random.randint(jax.random.fold_in(own, 2), (rows, 1), 0, top)
    return jnp.take_along_axis(grid, (jnp.arange(top)[None, :] + rotation) % top, axis=1)


def load_shares(count, total, most, lean, full):
    loads = [(1 << 20) // math.isqrt(standing ** lean) + 1 for standing in range(1, count + 1)]
    largest = most if full else min(most, max(-(-total // count), total * loads[0] // sum(loads)))
    least = 1 if total - largest >= count - 1 else 0
    given, surplus = [largest] + [least] * (count - 1), total - largest - least * (count - 1)
    while surplus > 0:
        candidates = [i for i in range(1, count) if given[i] < largest] or [i for i in range(1, count) if given[i] < most]
        whole, left = sum([loads[i] for i in candidates]), surplus
        for i in candidates:
            extra = min(most - given[i], max(1, left * loads[i] // whole), surplus)
            given[i] = given[i] + extra
            surplus = surplus - extra
    return np.array(given)


def bell_draw(own_key, extent, deviation, limit, cuts=(), held_as=jnp.bfloat16):
    result = jax.random.normal(own_key, extent, jnp.float32) * deviation
    if len(cuts) > 0:
        result = block_levels(own_key, extent, cuts, -0.22, 0.18) * result
    return jnp.clip(result, min=-limit, max=limit).astype(held_as)


def heavy_noise(key, shape, width, most, cuts, heavy, kind=jnp.bfloat16):
    values = width * jax.random.normal(key, shape, jnp.float32)
    if cuts:
        values = values * block_levels(key, shape, cuts, -0.22, 0.18)
    return jnp.clip(with_spikes(values, jax.random.fold_in(key, 3), *heavy), -most, most).astype(kind)


def setup_inputs(seed: int = 0) -> dict:
    arg_keys = jax.random.split(jax.random.key(seed), 9)
    queries = draw_queries(jax.random.fold_in(arg_keys[8], 71), 0)
    row_prompt_keys = jax.random.split(jax.random.fold_in(arg_keys[1], 1), ROWS // ROW_GRP)
    row_prompt_turns = jax.random.permutation(jax.random.fold_in(arg_keys[1], 3), ROWS // ROW_GRP)
    row_prompt = jax.vmap(lambda own, number: deal_out(jax.random.fold_in(arg_keys[1], 2), own, number, ROW_GRP, PROMPTS, 1, CAP, 2))(row_prompt_keys, row_prompt_turns).reshape((ROWS, 1))
    prompt_prefix_keys = draw_prompt_prefix_keys(jax.random.fold_in(arg_keys[8], 71), 0)
    prompt_prefix_values = bell_draw(arg_keys[3], (PROMPTS, PREFIX, KVW), 1.0, 6.0, ((0, 16), (1, 32)))
    row_suffix_keys = bell_draw(arg_keys[4], (ROWS, SUFFIX_SLOTS, KVW), 3.2, 12.0, ((0, 512),))
    row_suffix_values = bell_draw(arg_keys[5], (ROWS, SUFFIX_SLOTS, KVW), 1.0, 6.0, ((0, 512),))
    suffix_lengths = draw_suffix_lengths(jax.random.fold_in(arg_keys[8], 71), 0)
    w_out = heavy_noise(arg_keys[7], (QUERY_WIDTH, D), (QUERY_WIDTH // 16) ** -0.5, 0.75, ((0, 32),), (0, 1, 32, 2.75))
    return dict(queries=queries, row_prompt=row_prompt, prompt_prefix_keys=prompt_prefix_keys, prompt_prefix_values=prompt_prefix_values, row_suffix_keys=row_suffix_keys, row_suffix_values=row_suffix_values, suffix_lengths=suffix_lengths, w_out=w_out)


def attend_one_head(query_heads, key_rows, value_rows, valid):
    scores = jnp.dot(query_heads, key_rows.T, preferred_element_type=jnp.float32) / math.sqrt(HEAD_SIZE)
    scores = jnp.where(valid[None, :], scores, -1e+30)
    top = lax.optimization_barrier(jnp.max(scores, axis=1))
    weights = jnp.where(valid[None, :], jnp.exp(scores - top[:, None]), 0.0).astype(jnp.bfloat16)
    total = lax.optimization_barrier(jnp.sum(weights.astype(jnp.float32), axis=1))
    summed = jnp.dot(weights, value_rows, preferred_element_type=jnp.float32)
    return (top, total, summed)

def reference(queries, row_prompt, prompt_prefix_keys, prompt_prefix_values, row_suffix_keys, row_suffix_values, suffix_lengths, w_out):
    head_group = QUERY_HEADS // KEY_VALUE_HEADS
    prefix_valid = jnp.ones((PREFIX,), dtype=bool)

    def one_row(item_list):
        query_vector, prompt_index, suffix_key_rows, suffix_value_rows, suffix_length = item_list
        pkeys = lax.dynamic_index_in_dim(prompt_prefix_keys, prompt_index.astype(jnp.int32), 0, keepdims=False)
        pvalues = lax.dynamic_index_in_dim(prompt_prefix_values, prompt_index.astype(jnp.int32), 0, keepdims=False)
        suffix_mask = jnp.arange(SUFFIX_SLOTS, dtype=jnp.int32) < suffix_length
        pieces = []
        for head_index in range(KEY_VALUE_HEADS):
            column_span = slice(head_index * HEAD_SIZE, (head_index + 1) * HEAD_SIZE)
            query_head = query_vector[head_index * head_group * HEAD_SIZE:(head_index + 1) * head_group * HEAD_SIZE].reshape(head_group, HEAD_SIZE)
            ptop, ptotal, pout = attend_one_head(query_head, pkeys[:, column_span], pvalues[:, column_span], prefix_valid)
            stop_position, suffix_denominator, suffix_result = attend_one_head(query_head, suffix_key_rows[:, column_span], suffix_value_rows[:, column_span], suffix_mask)
            peak = jnp.maximum(ptop, stop_position)
            left = jnp.exp(ptop - peak)
            right = jnp.exp(stop_position - peak)
            numer = pout * left[:, None] + suffix_result * right[:, None]
            denom = ptotal * left + suffix_denominator * right
            pieces.append((numer / denom[:, None]).reshape(head_group * HEAD_SIZE))
        return jnp.concatenate(pieces).astype(jnp.bfloat16)
    attended = lax.map(one_row, (queries, row_prompt[:, 0], row_suffix_keys, row_suffix_values, suffix_lengths))
    return jnp.dot(attended, w_out, preferred_element_type=jnp.float32).astype(jnp.bfloat16)
```

```python
import math

import jax
import jax.numpy as jnp
from jax import lax
from jax.experimental import pallas as pl
from jax.experimental.pallas import tpu as pltpu
from jax.sharding import Mesh, PartitionSpec as P

QUERY_HEADS = 32
KEY_VALUE_HEADS = 4
HEAD_SIZE = 128
SUFFIX_SLOTS = 128
CAP = 8
PLANE = ("x", "y")
SWAP = ((0, 1), (1, 0))
TAIL = 16
FACTOR = 1.0 / math.sqrt(HEAD_SIZE)
LOG2E = 1.0 / math.log(2.0)
BIG = 48 * 1024 * 1024
F32, BF16 = jnp.float32, jnp.bfloat16


def iota(shape, dim):
    return lax.broadcasted_iota(jnp.int32, shape, dim)


def matmul(a, b, ca=1, cb=0):
    return lax.dot_general(a, b, (((ca,), (cb,)), ((), ())), preferred_element_type=F32)


def high_part(value):
    return value.astype(BF16).astype(F32)


def whole_spec(shape):
    return pl.BlockSpec(shape, lambda *_: (0,) * len(shape))


def pack_kernel(prompt_ref, query_ref, packed_ref, place_ref):
    prompt = prompt_ref[...]
    rows, slots = prompt.shape[0], packed_ref.shape[0]
    lanes = iota((rows, slots), 1)
    named = (lanes == prompt).astype(F32)
    lower = (iota((rows, rows), 0) > iota((rows, rows), 1)).astype(F32)
    before = matmul(lower.astype(BF16), named.astype(BF16))
    rank = jnp.sum(before * named, axis=1, keepdims=True).astype(jnp.int32)
    place = (lanes == prompt * CAP + rank).astype(F32).astype(BF16)
    place_ref[...] = place
    packed_ref[...] = matmul(place, query_ref[...], 0, 0).astype(BF16)


def pack(row_prompt, queries, slots):
    rows = queries.shape[0]
    return pl.pallas_call(
        pack_kernel,
        out_shape=(
            jax.ShapeDtypeStruct((slots, HEAD_SIZE), BF16),
            jax.ShapeDtypeStruct((rows, slots), BF16),
        ),
        name="pack",
    )(row_prompt, queries)


def attend_kernel(
    core_ref,
    own_len_ref,
    other_len_ref,
    here_ref,
    k0_ref,
    k1_ref,
    v0_ref,
    v1_ref,
    sk0_ref,
    sk1_ref,
    sv0_ref,
    sv1_ref,
    out_ref,
):
    heads = here_ref.shape[0]
    slots = here_ref.shape[1] - TAIL
    ones = jnp.ones((k0_ref.shape[0], HEAD_SIZE), BF16)
    v0 = jnp.concatenate([v0_ref[...], ones], axis=1)
    v1 = jnp.concatenate([v1_ref[...], ones], axis=1)
    k0, k1 = k0_ref[...], k1_ref[...]

    rows = heads * TAIL
    suffix_query = jnp.concatenate([here_ref[h, slots:, :] for h in range(heads)], axis=0)
    skeys = jnp.concatenate([sk0_ref[0], sk0_ref[1], sk1_ref[0], sk1_ref[1]], axis=0)
    svalues = jnp.concatenate([sv0_ref[0], sv0_ref[1], sv1_ref[0], sv1_ref[1]], axis=0)
    span = skeys.shape[0]
    scores = matmul(suffix_query, skeys, 1, 1)
    column = iota((rows, span), 1)
    block, place = column >> 7, column & 127
    length = jnp.where(
        block < 2,
        jnp.where(block == 0, own_len_ref[0], own_len_ref[1]),
        jnp.where(block == 2, other_len_ref[0], other_len_ref[1]),
    )
    line = iota((rows, span), 0) & 7
    live = (line == ((block + 2 * core_ref[0]) & 3)) & (place < length)
    peak = jnp.max(jnp.where(live, scores, -1e30), axis=1, keepdims=True)
    sshift = high_part(peak * FACTOR)
    sweights = jnp.where(live, jnp.exp2(scores * (FACTOR * LOG2E) - sshift * LOG2E), 0.0)
    sweights = sweights.astype(BF16)
    souts = matmul(
        sweights, jnp.concatenate([svalues, jnp.ones((span, HEAD_SIZE), BF16)], axis=1)
    )
    lane = iota((rows, HEAD_SIZE), 1)
    stotal = souts[:, HEAD_SIZE:]
    stotal_high = high_part(stotal)
    numbers = jnp.where(
        lane == 0,
        sshift,
        jnp.where(lane == 1, stotal_high, jnp.where(lane == 2, stotal - stotal_high, 0.0)),
    )
    tail_line = iota((rows, HEAD_SIZE), 0) & (TAIL - 1)
    tail = jnp.where(
        tail_line < 4,
        souts[:, :HEAD_SIZE],
        jnp.where((tail_line >= 8) & (tail_line < 12), numbers, 0.0),
    )

    lane = iota((2 * slots, HEAD_SIZE), 1)
    for pair in range(heads // 2):
        query = jnp.concatenate([here_ref[2 * pair + i, :slots, :] for i in range(2)], axis=0)
        s0 = matmul(query, k0, 1, 1)
        s1 = matmul(query, k1, 1, 1)
        peak = jnp.maximum(
            jnp.max(s0, axis=1, keepdims=True), jnp.max(s1, axis=1, keepdims=True)
        )
        shift = high_part(peak * FACTOR)
        low = shift * LOG2E
        w0 = jnp.exp2(s0 * (FACTOR * LOG2E) - low).astype(BF16)
        w1 = jnp.exp2(s1 * (FACTOR * LOG2E) - low).astype(BF16)
        outs = matmul(w0, v0) + matmul(w1, v1)
        total = outs[:, HEAD_SIZE:]
        total_high = high_part(total)
        numbers = jnp.where(
            lane == 4,
            shift,
            jnp.where(lane == 5, total_high, jnp.where(lane == 6, total - total_high, 0.0)),
        )
        for i in range(2):
            h = 2 * pair + i
            cut = slice(i * slots, (i + 1) * slots)
            out_ref[h, :slots, :] = outs[cut, :HEAD_SIZE].astype(BF16)
            across = numbers[cut].T[:TAIL]
            out_ref[h, slots:, :] = (tail[h * TAIL : (h + 1) * TAIL] + across).astype(BF16)


def attend(core, own_len, other_len, here, k0, k1, v0, v1, sk0, sk1, sv0, sv1):
    chips, height, _ = here.shape
    heads = chips // KEY_VALUE_HEADS
    length = k0.shape[0]
    smem = pl.BlockSpec(memory_space=pltpu.SMEM)
    chunk = pl.BlockSpec((heads, height, HEAD_SIZE), lambda j: (j, 0, 0))
    prefix = pl.BlockSpec((length, HEAD_SIZE), lambda j: (0, j))
    suffix = pl.BlockSpec((2, SUFFIX_SLOTS, HEAD_SIZE), lambda j: (0, 0, j))
    return pl.pallas_call(
        attend_kernel,
        grid=(KEY_VALUE_HEADS,),
        in_specs=[smem, smem, smem, chunk] + [prefix] * 4 + [suffix] * 4,
        out_specs=chunk,
        out_shape=jax.ShapeDtypeStruct(here.shape, BF16),
        compiler_params=pltpu.CompilerParams(vmem_limit_bytes=BIG),
        cost_estimate=pl.CostEstimate(
            flops=4 * chips * height * 2 * length * HEAD_SIZE,
            bytes_accessed=10 * length * KEY_VALUE_HEADS * HEAD_SIZE,
            transcendentals=chips * height * 2 * length,
        ),
        name="attend",
    )(core, own_len, other_len, here, k0, k1, v0, v1, sk0, sk1, sv0, sv1)


def merge_kernel(own_ref, sent_ref):
    chips, height, _ = own_ref.shape
    slots, groups = height - TAIL, sent_ref.shape[0]
    tails = own_ref[:, slots:, :].astype(F32)
    shift = tails[:, 4, :]
    total = tails[:, 5, :] + tails[:, 6, :]
    top = jnp.max(shift, axis=0, keepdims=True)
    scale = jnp.exp(shift - top)
    whole = jnp.sum(total * scale, axis=0, keepdims=True)
    whole_high = high_part(whole)
    line = iota((8, slots), 0)
    numbers = jnp.where(
        line == 0, top, jnp.where(line == 1, whole_high, jnp.where(line == 2, whole - whole_high, 0.0))
    )
    rest = jnp.zeros((HEAD_SIZE - chips - 8, slots), F32)
    across = jnp.concatenate([scale / whole, numbers, rest], axis=0).T
    mean = jnp.zeros((slots, HEAD_SIZE), F32)
    for k in range(chips):
        mean += across[:, k : k + 1] * own_ref[k, :slots, :].astype(F32)
    cap = slots // groups
    both = [value.reshape(groups, cap, HEAD_SIZE) for value in (mean, across)]
    sent_ref[...] = jnp.concatenate(both, axis=1).astype(BF16)


def merge(own, groups):
    cap = (own.shape[1] - TAIL) // groups
    return pl.pallas_call(
        merge_kernel,
        out_shape=jax.ShapeDtypeStruct((groups, 2 * cap, HEAD_SIZE), BF16),
        compiler_params=pltpu.CompilerParams(vmem_limit_bytes=BIG),
        name="merge",
    )(own)


def finish_kernel(first, place_ref, back_ref, tails_ref, attended_ref):
    groups, double, _ = back_ref.shape
    cap = double // 2
    rows = place_ref.shape[0]
    chips = tails_ref.shape[0]
    back = back_ref[...].astype(F32)
    means = back[:, :cap].reshape(groups * cap, HEAD_SIZE).astype(BF16)
    numbers = back[:, cap:].reshape(groups * cap, HEAD_SIZE).astype(BF16)
    place = place_ref[...]
    pre_mean = matmul(place, means)
    pre_numbers = matmul(place, numbers)
    pre_top = pre_numbers[:, first : first + 1]
    pre_total = pre_numbers[:, first + 1 : first + 2] + pre_numbers[:, first + 2 : first + 3]

    tails = tails_ref[...].reshape(chips * TAIL, HEAD_SIZE)
    row, column = iota((rows, chips * TAIL), 0), iota((rows, chips * TAIL), 1)
    spot = (row >> 2) * TAIL + (row & 3)
    suf_out = matmul((column == spot).astype(F32).astype(BF16), tails)
    suf_numbers = matmul((column == spot + 8).astype(F32).astype(BF16), tails)
    suf_top = suf_numbers[:, 0:1]
    suf_total = suf_numbers[:, 1:2] + suf_numbers[:, 2:3]

    peak = jnp.maximum(pre_top, suf_top)
    left = jnp.exp(pre_top - peak) * pre_total
    right = jnp.exp(suf_top - peak)
    attended = (pre_mean * left + suf_out * right) / (left + suf_total * right)
    attended_ref[...] = attended.astype(BF16)


def finish(place, back, own):
    chips, height, _ = own.shape
    rows = place.shape[0]
    return pl.pallas_call(
        lambda *refs: finish_kernel(chips, *refs),
        grid=(1,),
        in_specs=[
            whole_spec(place.shape),
            whole_spec(back.shape),
            pl.BlockSpec((chips, TAIL, HEAD_SIZE), lambda i: (0, height // TAIL - 1, 0)),
        ],
        out_specs=whole_spec((rows, HEAD_SIZE)),
        out_shape=jax.ShapeDtypeStruct((rows, HEAD_SIZE), BF16),
        name="finish",
    )(place, back, own)


def project_kernel(core_ref, a0_ref, a1_ref, w0_ref, w1_ref, out_ref):
    width = out_ref.shape[2]
    a0, a1 = a0_ref[...], a1_ref[...]
    for k in range(out_ref.shape[0]):
        start = pl.multiple_of(2 * width * k + core_ref[0] * width, width)
        columns = pl.ds(start, width)
        out_ref[k] = (matmul(a0, w0_ref[:, columns]) + matmul(a1, w1_ref[:, columns])).astype(BF16)


def project(core, a0, a1, w0, w1, chips):
    rows, feats = a0.shape
    width = w0.shape[1] // (2 * chips)
    steps = 2
    part = chips // steps
    weight = pl.BlockSpec((feats, 2 * width * part), lambda i: (0, i))
    return pl.pallas_call(
        project_kernel,
        grid=(steps,),
        in_specs=[
            pl.BlockSpec(memory_space=pltpu.SMEM),
            whole_spec(a0.shape),
            whole_spec(a1.shape),
            weight,
            weight,
        ],
        out_specs=pl.BlockSpec((part, rows, width), lambda i: (i, 0, 0)),
        out_shape=jax.ShapeDtypeStruct((chips, rows, width), BF16),
        compiler_params=pltpu.CompilerParams(vmem_limit_bytes=BIG),
        name="project",
    )(core, a0, a1, w0, w1)


def body(
    queries,
    row_prompt,
    prompt_prefix_keys,
    prompt_prefix_values,
    row_suffix_keys,
    row_suffix_values,
    suffix_lengths,
    w_out,
):
    groups = lax.axis_size("grp")
    chips = lax.axis_size("x") * lax.axis_size("y")
    core = lax.axis_index("core").reshape(1).astype(jnp.int32)
    row_grp = queries.shape[0]
    chip_rows = row_grp // chips
    slots = groups * CAP
    keys, values = prompt_prefix_keys[0], prompt_prefix_values[0]

    packed, place = pack(row_prompt, queries, slots)
    arrived = lax.all_to_all(packed, "grp", split_axis=0, concat_axis=0, tiled=True)

    held = (keys, values, row_suffix_keys, row_suffix_values, suffix_lengths, w_out)
    _, held = lax.optimization_barrier((packed, held))
    others = [lax.ppermute(value, "core", SWAP) for value in held]
    keys_other, values_other, skeys_other, svalues_other, lengths_other, w_other = others

    asked = queries.reshape(chips, chip_rows, HEAD_SIZE)
    gap = jnp.zeros((chips, 8 - chip_rows, HEAD_SIZE), BF16)
    spread = jnp.concatenate(
        [jnp.broadcast_to(arrived[None], (chips, slots, HEAD_SIZE)), asked, gap, asked, gap],
        axis=1,
    )
    here = lax.all_to_all(spread, PLANE, split_axis=0, concat_axis=0, tiled=True)

    parts = attend(
        core,
        suffix_lengths,
        lengths_other,
        here,
        keys,
        keys_other,
        values,
        values_other,
        row_suffix_keys,
        skeys_other,
        row_suffix_values,
        svalues_other,
    )
    own = lax.all_to_all(parts, PLANE, split_axis=0, concat_axis=0, tiled=True)

    sent = merge(own, groups)
    back = lax.all_to_all(sent, "grp", split_axis=0, concat_axis=0, tiled=True)
    attended = finish(place, back, own)
    attended_other = lax.ppermute(attended, "core", SWAP)
    shares = project(core, attended, attended_other, w_out, w_other, chips)
    shares = lax.all_to_all(shares, PLANE, split_axis=0, concat_axis=0, tiled=True)
    return jnp.sum(shares.astype(F32), axis=0).astype(BF16)


def solution(mesh):
    side = math.isqrt(mesh.shape["seq"] // 2)
    fine = Mesh(
        mesh.devices.reshape(mesh.shape["grp"], side, side, 2), ("grp", "x", "y", "core")
    )
    seq = ("x", "y", "core")
    every = ("grp",) + seq
    in_specs = (
        P("grp", seq),
        P("grp", None),
        P("grp", seq, None),
        P("grp", seq, None),
        P(every, None, None),
        P(every, None, None),
        P(every),
        P(seq, None),
    )
    return jax.shard_map(
        body, mesh=fine, in_specs=in_specs, out_specs=P("grp", seq), check_vma=False
    )
```

```python
import math

import jax
import jax.numpy as jnp
from jax import lax
from jax.experimental import pallas as pl
from jax.experimental.pallas import tpu as pltpu
from jax.sharding import Mesh, PartitionSpec as P

QUERY_HEADS = 32
KEY_VALUE_HEADS = 4
HEAD_SIZE = 128
SUFFIX_SLOTS = 128
CAP = 8
PLANE = ("x", "y")
SWAP = ((0, 1), (1, 0))
TAIL = 16
FACTOR = 1.0 / math.sqrt(HEAD_SIZE)
LOG2E = 1.0 / math.log(2.0)
BIG = 28 * 1024 * 1024
MOST = 58 * 1024 * 1024
F32, BF16 = jnp.float32, jnp.bfloat16


def iota(shape, dim):
    return lax.broadcasted_iota(jnp.int32, shape, dim)


def matmul(a, b, ca=1, cb=0):
    return lax.dot_general(a, b, (((ca,), (cb,)), ((), ())), preferred_element_type=F32)


def high_part(value):
    return value.astype(BF16).astype(F32)


def whole_spec(shape):
    return pl.BlockSpec(shape, lambda *_: (0,) * len(shape))


HBM = pl.BlockSpec(memory_space=pltpu.HBM)
SMEM = pl.BlockSpec(memory_space=pltpu.SMEM)
VMEM = pl.BlockSpec(memory_space=pltpu.VMEM)
PIECES = 4


def layout_of(length, chips, feats, wide, suffix_rows):
    weights = 2 * length
    skeys = weights + chips * feats // 2
    svalues = skeys + suffix_rows
    lengths = svalues + suffix_rows
    return 0, length, weights, skeys, svalues, lengths, lengths + TAIL


def pack_kernel(
    core_ref,
    len_ref,
    prompt_ref,
    query_ref,
    k_ref,
    v_ref,
    sk_ref,
    sv_ref,
    w_ref,
    packed_ref,
    place_ref,
    tails_ref,
    bundle_ref,
    stage_ref,
    in_sems,
    out_sems,
):
    length, wide = k_ref.shape
    feats, chips = w_ref.shape[0], tails_ref.shape[0] // TAIL
    width = w_ref.shape[1] // (2 * chips)
    spots = layout_of(length, chips, feats, wide, sk_ref.shape[0])
    moves = []

    def move(source, rows, columns):
        copy = pltpu.make_async_copy(
            source, stage_ref.at[rows, columns], in_sems.at[len(moves)]
        )
        copy.start()
        moves.append((copy, rows, columns))

    piece = length // PIECES
    every = pl.ds(0, wide)
    for ref, first in ((k_ref, spots[0]), (v_ref, spots[1])):
        for i in range(PIECES):
            move(ref.at[pl.ds(i * piece, piece), :], pl.ds(first + i * piece, piece), every)
    other = 1 - core_ref[0]
    for k in range(chips):
        columns = pl.ds(pl.multiple_of(2 * width * k + other * width, width), width)
        rows = pl.ds(spots[2] + (k // 2) * feats, feats)
        move(w_ref.at[:, columns], rows, pl.ds((k % 2) * width, width))
    for ref, first in ((sk_ref, spots[3]), (sv_ref, spots[4])):
        move(ref, pl.ds(first, ref.shape[0]), every)
    line = iota((TAIL, wide), 0)
    lengths = jnp.where(line == 0, len_ref[0], jnp.where(line == 1, len_ref[1], 0))
    stage_ref[spots[5] :, :] = lengths.astype(F32).astype(BF16)

    prompt = prompt_ref[...]
    slots, rows = place_ref.shape
    lines = iota((slots, rows), 0)
    named = (lines == prompt).astype(F32)
    earlier = (iota((rows, rows), 0) < iota((rows, rows), 1)).astype(F32)
    before = matmul(named.astype(BF16), earlier.astype(BF16))
    rank = jnp.sum(before * named, axis=0, keepdims=True).astype(jnp.int32)
    place = (lines == prompt * CAP + rank).astype(F32).astype(BF16)
    place_ref[...] = place
    query = query_ref[...]
    packed_ref[...] = matmul(place, query).astype(BF16)

    line, row = iota((chips * TAIL, rows), 0), iota((chips * TAIL, rows), 1)
    spot = line & 7
    asks = (spot < 4) & (row == (line >> 4) * 4 + spot)
    tails_ref[...] = matmul(asks.astype(F32).astype(BF16), query).astype(BF16)

    leaving = []

    def leave(rows, columns):
        copy = pltpu.make_async_copy(
            stage_ref.at[rows, columns], bundle_ref.at[rows, columns], out_sems.at[len(leaving)]
        )
        copy.start()
        leaving.append(copy)

    leave(pl.ds(spots[5], TAIL), every)
    for copy, rows, columns in moves:
        copy.wait()
        leave(rows, columns)
    for copy in leaving:
        copy.wait()


def pack(core, lengths, prompt, queries, keys, values, skeys, svalues, w, slots, chips):
    rows = queries.shape[0]
    length, wide = keys.shape
    height = layout_of(length, chips, w.shape[0], wide, skeys.shape[0])[-1]
    return pl.pallas_call(
        pack_kernel,
        in_specs=[SMEM, SMEM, VMEM, VMEM] + [HBM] * 5,
        out_specs=(VMEM, VMEM, VMEM, HBM),
        out_shape=(
            jax.ShapeDtypeStruct((slots, HEAD_SIZE), BF16),
            jax.ShapeDtypeStruct((slots, rows), BF16),
            jax.ShapeDtypeStruct((chips * TAIL, HEAD_SIZE), BF16),
            jax.ShapeDtypeStruct((height, wide), BF16),
        ),
        scratch_shapes=[
            pltpu.VMEM((height, wide), BF16),
            pltpu.SemaphoreType.DMA((2 * PIECES + chips + 2,)),
            pltpu.SemaphoreType.DMA((2 * PIECES + chips + 3,)),
        ],
        compiler_params=pltpu.CompilerParams(vmem_limit_bytes=MOST),
        name="pack",
    )(core, lengths, prompt, queries, keys, values, skeys, svalues, w)


def spread_kernel(arrived_ref, tails_ref, out_ref):
    chips, height, _ = out_ref.shape
    arrived = arrived_ref[...]
    for k in range(chips):
        out_ref[k, : height - TAIL, :] = arrived
        out_ref[k, height - TAIL :, :] = tails_ref[k * TAIL : (k + 1) * TAIL]


def spread(arrived, tails, chips):
    return pl.pallas_call(
        spread_kernel,
        out_shape=jax.ShapeDtypeStruct((chips, arrived.shape[0] + TAIL, HEAD_SIZE), BF16),
        compiler_params=pltpu.CompilerParams(vmem_limit_bytes=BIG),
        name="spread",
    )(arrived, tails)


def suffix_part(core, lengths, query, keys, values):
    rows, span = query.shape[0], keys.shape[0]
    scores = matmul(query, keys, 1, 1)
    column = iota((rows, span), 1)
    block, place = column >> 7, column & 127
    live = ((iota((rows, span), 0) & 7) == ((block + 2 * core) & 3)) & (place < lengths)
    peak = jnp.max(jnp.where(live, scores, -1e30), axis=1, keepdims=True)
    shift = high_part(peak * FACTOR)
    weights = jnp.where(live, jnp.exp2(scores * (FACTOR * LOG2E) - shift * LOG2E), 0.0)
    ones = jnp.ones((span, HEAD_SIZE), BF16)
    outs = matmul(weights.astype(BF16), jnp.concatenate([values, ones], axis=1))
    lane = iota((rows, HEAD_SIZE), 1)
    total = outs[:, HEAD_SIZE:]
    total_high = high_part(total)
    numbers = jnp.where(
        lane == 0,
        shift,
        jnp.where(lane == 1, total_high, jnp.where(lane == 2, total - total_high, 0.0)),
    )
    line = iota((rows, HEAD_SIZE), 0) & (TAIL - 1)
    return jnp.where(
        line < 4, outs[:, :HEAD_SIZE], jnp.where((line >= 8) & (line < 12), numbers, 0.0)
    )


def attend_kernel(
    core_ref,
    len_ref,
    here_ref,
    k_ref,
    v_ref,
    sk_ref,
    sv_ref,
    bundle_ref,
    out_ref,
    w_ref,
    k_buf,
    v_buf,
    sk_buf,
    sv_buf,
    len_buf,
    even_ref,
    odd_ref,
    sems,
):
    step = pl.program_id(0)
    steps = k_buf.shape[0]
    total_heads = here_ref.shape[0]
    slots = here_ref.shape[1] - TAIL
    length, wide = k_ref.shape
    chips = total_heads * steps
    own_suffix = sk_ref.shape[0]
    spots = layout_of(length, chips, HEAD_SIZE, wide, own_suffix)
    part = wide // steps
    kv_heads = part // HEAD_SIZE
    heads = total_heads // kv_heads
    parts = (
        (k_ref, spots[0], length, k_buf),
        (v_ref, spots[1], length, v_buf),
        (sk_ref, spots[3], own_suffix, sk_buf),
        (sv_ref, spots[4], own_suffix, sv_buf),
    )

    def copies(i, s):
        ref, first, count, buf = parts[i]
        columns = pl.ds(pl.multiple_of(s * part, part), part)
        return (
            pltpu.make_async_copy(
                ref.at[:, columns], buf.at[s, pl.ds(0, count)], sems.at[s, 2 * i]
            ),
            pltpu.make_async_copy(
                bundle_ref.at[pl.ds(first, count), columns],
                buf.at[s, pl.ds(count, count)],
                sems.at[s, 2 * i + 1],
            ),
        )

    len_copy = pltpu.make_async_copy(
        bundle_ref.at[pl.ds(spots[5], TAIL), :], len_buf, sems.at[0, 2 * len(parts)]
    )

    w_copy = pltpu.make_async_copy(
        bundle_ref.at[pl.ds(spots[2], w_ref.shape[0]), :], w_ref, sems.at[1, 2 * len(parts)]
    )

    @pl.when(step == 0)
    def _():
        for s in range(steps):
            for i in (0, 2, 3, 1):
                for copy in copies(i, s):
                    copy.start()
            if s == 0:
                len_copy.start()
        w_copy.start()
        len_copy.wait()

    def arrive(i):
        for copy in copies(i, step):
            copy.wait()

    cuts = [slice(j * HEAD_SIZE, (j + 1) * HEAD_SIZE) for j in range(kv_heads)]
    ones = jnp.ones((2 * length, HEAD_SIZE), BF16)
    held = (even_ref, odd_ref)
    units = [(j, j * heads + 2 * p) for j in range(kv_heads) for p in range(heads // 2)]

    def scores(unit):
        j, first = units[unit]
        query = jnp.concatenate([here_ref[first + i, :slots, :] for i in range(2)], axis=0)
        value = matmul(query, k_buf[step, :, cuts[j]], 1, 1)
        held[unit % 2][...] = value
        return jnp.max(value, axis=1, keepdims=True)

    arrive(0)
    peak = scores(0)
    arrive(2)
    arrive(3)
    span = 2 * own_suffix
    block = iota((1, span), 1) >> 7
    others = len_buf[...].astype(F32)
    pick = lambda row: others[row : row + 1, :HEAD_SIZE].astype(jnp.int32)
    fixed = lambda row: jnp.full((1, HEAD_SIZE), len_ref[row], jnp.int32)
    lengths = jnp.concatenate([fixed(0), fixed(1), pick(0), pick(1)], axis=1)
    tails = []
    for j in range(kv_heads):
        asks = jnp.concatenate([here_ref[j * heads + h, slots:, :] for h in range(heads)], axis=0)
        tails.append(
            suffix_part(
                core_ref[0], lengths, asks, sk_buf[step, :, cuts[j]], sv_buf[step, :, cuts[j]]
            )
        )
    arrive(1)

    lane = iota((2 * slots, HEAD_SIZE), 1)
    for unit, (j, start) in enumerate(units):
        peak_next = scores(unit + 1) if unit + 1 < len(units) else None
        shift = high_part(peak * FACTOR)
        weights = jnp.exp2(held[unit % 2][...] * (FACTOR * LOG2E) - shift * LOG2E).astype(BF16)
        outs = matmul(weights, jnp.concatenate([v_buf[step, :, cuts[j]], ones], axis=1))
        total = outs[:, HEAD_SIZE:]
        total_high = high_part(total)
        numbers = jnp.where(
            lane == 4,
            shift,
            jnp.where(lane == 5, total_high, jnp.where(lane == 6, total - total_high, 0.0)),
        )
        for i in range(2):
            h = start + i
            cut = slice(i * slots, (i + 1) * slots)
            out_ref[h, :slots, :] = outs[cut, :HEAD_SIZE].astype(BF16)
            place = (h - j * heads) * TAIL
            tail = tails[j][place : place + TAIL] + numbers[cut].T[:TAIL]
            out_ref[h, slots:, :] = tail.astype(BF16)
        peak = peak_next

    @pl.when(step == steps - 1)
    def _():
        w_copy.wait()


def attend(core, lengths, here, keys, values, skeys, svalues, bundle):
    chips, height, _ = here.shape
    steps = 2
    heads = chips // steps
    length, wide = keys.shape
    part = wide // steps
    slots, own_suffix = height - TAIL, skeys.shape[0]
    chunk = pl.BlockSpec((heads, height, HEAD_SIZE), lambda j: (j, 0, 0))
    return pl.pallas_call(
        attend_kernel,
        grid=(steps,),
        in_specs=[SMEM, SMEM, chunk] + [HBM] * 5,
        out_specs=(chunk, whole_spec((chips * HEAD_SIZE // 2, wide))),
        out_shape=(
            jax.ShapeDtypeStruct(here.shape, BF16),
            jax.ShapeDtypeStruct((chips * HEAD_SIZE // 2, wide), BF16),
        ),
        scratch_shapes=[
            pltpu.VMEM((steps, 2 * length, part), BF16),
            pltpu.VMEM((steps, 2 * length, part), BF16),
            pltpu.VMEM((steps, 2 * own_suffix, part), BF16),
            pltpu.VMEM((steps, 2 * own_suffix, part), BF16),
            pltpu.VMEM((TAIL, wide), BF16),
            pltpu.VMEM((2 * slots, 2 * length), F32),
            pltpu.VMEM((2 * slots, 2 * length), F32),
            pltpu.SemaphoreType.DMA((steps, 9)),
        ],
        compiler_params=pltpu.CompilerParams(vmem_limit_bytes=36 * 1024 * 1024),
        cost_estimate=pl.CostEstimate(
            flops=8 * chips * height * length * HEAD_SIZE,
            bytes_accessed=10 * length * wide,
            transcendentals=2 * chips * height * length,
        ),
        name="attend",
    )(core, lengths, here, keys, values, skeys, svalues, bundle)


def merge_kernel(own_ref, sent_ref):
    chips, height, _ = own_ref.shape
    slots, groups = height - TAIL, sent_ref.shape[0]
    tails = own_ref[:, slots:, :].astype(F32)
    shift = tails[:, 4, :]
    total = tails[:, 5, :] + tails[:, 6, :]
    top = jnp.max(shift, axis=0, keepdims=True)
    scale = jnp.exp(shift - top)
    whole = jnp.sum(total * scale, axis=0, keepdims=True)
    whole_high = high_part(whole)
    line = iota((8, slots), 0)
    numbers = jnp.where(
        line == 0, top, jnp.where(line == 1, whole_high, jnp.where(line == 2, whole - whole_high, 0.0))
    )
    rest = jnp.zeros((HEAD_SIZE - chips - 8, slots), F32)
    across = jnp.concatenate([scale / whole, numbers, rest], axis=0).T
    mean = jnp.zeros((slots, HEAD_SIZE), F32)
    for k in range(chips):
        mean += across[:, k : k + 1] * own_ref[k, :slots, :].astype(F32)
    cap = slots // groups
    both = [value.reshape(groups, cap, HEAD_SIZE) for value in (mean, across)]
    sent_ref[...] = jnp.concatenate(both, axis=1).astype(BF16)


def merge(own, groups):
    chips, height, _ = own.shape
    cap = (height - TAIL) // groups
    return pl.pallas_call(
        merge_kernel,
        out_shape=jax.ShapeDtypeStruct((groups, 2 * cap, HEAD_SIZE), BF16),
        compiler_params=pltpu.CompilerParams(vmem_limit_bytes=BIG),
        name="merge",
    )(own)


def finish_kernel(place_ref, back_ref, tails_ref, out_ref):
    groups, double, _ = back_ref.shape
    cap, rows = double // 2, place_ref.shape[1]
    chips = tails_ref.shape[0]
    span = chips * TAIL
    back = back_ref[...].astype(F32)
    means = back[:, :cap].reshape(groups * cap, HEAD_SIZE).astype(BF16)
    numbers = back[:, cap:].reshape(groups * cap, HEAD_SIZE).astype(BF16)
    both = matmul(place_ref[...], jnp.concatenate([means, numbers], axis=1), 0, 0)
    pre_mean, pre_numbers = both[:, :HEAD_SIZE], both[:, HEAD_SIZE:]
    pre_top = pre_numbers[:, chips : chips + 1]
    pre_total = pre_numbers[:, chips + 1 : chips + 2] + pre_numbers[:, chips + 2 : chips + 3]

    tails = tails_ref[...].reshape(span, HEAD_SIZE)
    line, column = iota((2 * rows, span), 0), iota((2 * rows, span), 1)
    row = line & (rows - 1)
    spot = (row >> 2) * TAIL + (row & 3) + jnp.where(line < rows, 0, 8)
    picked = matmul((column == spot).astype(F32).astype(BF16), tails)
    suf_out, suf_numbers = picked[:rows], picked[rows:]
    suf_top = suf_numbers[:, 0:1]
    suf_total = suf_numbers[:, 1:2] + suf_numbers[:, 2:3]

    peak = jnp.maximum(pre_top, suf_top)
    left = jnp.exp(pre_top - peak) * pre_total
    right = jnp.exp(suf_top - peak)
    attended = (pre_mean * left + suf_out * right) / (left + suf_total * right)
    out_ref[...] = attended.astype(BF16)


def finish(place, back, own):
    chips, height, _ = own.shape
    rows = place.shape[1]
    return pl.pallas_call(
        finish_kernel,
        grid=(1,),
        in_specs=[
            whole_spec(place.shape),
            whole_spec(back.shape),
            pl.BlockSpec((chips, TAIL, HEAD_SIZE), lambda i: (0, height // TAIL - 1, 0)),
        ],
        out_specs=whole_spec((rows, HEAD_SIZE)),
        out_shape=jax.ShapeDtypeStruct((rows, HEAD_SIZE), BF16),
        name="finish",
    )(place, back, own)


def project_kernel(core_ref, a_ref, w0_ref, w1_ref, out_ref):
    width = out_ref.shape[2]
    feats = w0_ref.shape[0]
    core = core_ref[0]
    attended = jnp.concatenate([a_ref[core], a_ref[1 - core]], axis=1)
    for k in range(out_ref.shape[0]):
        own = w0_ref[:, pl.ds(pl.multiple_of(2 * width * k + core * width, width), width)]
        half, side = (k // 2) * feats, (k % 2) * width
        other = w1_ref[half : half + feats, side : side + width]
        out_ref[k] = matmul(attended, jnp.concatenate([own, other], axis=0)).astype(BF16)


def project(core, attended, w, w_other, chips):
    _, rows, feats = attended.shape
    width = w.shape[1] // (2 * chips)
    steps = 2
    part = chips // steps
    high = part * feats // 2
    return pl.pallas_call(
        project_kernel,
        grid=(steps,),
        in_specs=[
            SMEM,
            whole_spec(attended.shape),
            pl.BlockSpec((feats, 2 * width * part), lambda i: (0, i)),
            pl.BlockSpec((high, 2 * width), lambda i: (i, 0)),
        ],
        out_specs=pl.BlockSpec((part, rows, width), lambda i: (i, 0, 0)),
        out_shape=jax.ShapeDtypeStruct((chips, rows, width), BF16),
        compiler_params=pltpu.CompilerParams(vmem_limit_bytes=BIG),
        name="project",
    )(core, attended, w, w_other)


def body(
    queries,
    row_prompt,
    prompt_prefix_keys,
    prompt_prefix_values,
    row_suffix_keys,
    row_suffix_values,
    suffix_lengths,
    w_out,
):
    groups = lax.axis_size("grp")
    chips = lax.axis_size("x") * lax.axis_size("y")
    core = lax.axis_index("core").reshape(1).astype(jnp.int32)
    row_grp = queries.shape[0]
    slots = groups * CAP
    keys, values = prompt_prefix_keys[0], prompt_prefix_values[0]
    skeys = row_suffix_keys.reshape(-1, row_suffix_keys.shape[2])
    svalues = row_suffix_values.reshape(-1, row_suffix_values.shape[2])

    packed, place, tails, bundle = pack(
        core,
        suffix_lengths,
        row_prompt.reshape(1, row_grp),
        queries,
        keys,
        values,
        skeys,
        svalues,
        w_out,
        slots,
        chips,
    )
    bundle = lax.ppermute(bundle, "core", SWAP)
    arrived = lax.all_to_all(packed, "grp", split_axis=0, concat_axis=0, tiled=True)

    here = lax.all_to_all(
        spread(arrived, tails, chips), PLANE, split_axis=0, concat_axis=0, tiled=True
    )
    parts, w_other = attend(core, suffix_lengths, here, keys, values, skeys, svalues, bundle)
    own = lax.all_to_all(parts, PLANE, split_axis=0, concat_axis=0, tiled=True)

    sent = merge(own, groups)
    back = lax.all_to_all(sent, "grp", split_axis=0, concat_axis=0, tiled=True)
    attended = lax.all_gather(finish(place, back, own), "core", axis=0, tiled=False)
    shares = project(core, attended, w_out, w_other, chips)
    shares = lax.all_to_all(shares, PLANE, split_axis=0, concat_axis=0, tiled=True)
    return jnp.sum(shares.astype(F32), axis=0).astype(BF16)


def solution(mesh):
    side = math.isqrt(mesh.shape["seq"] // 2)
    fine = Mesh(
        mesh.devices.reshape(mesh.shape["grp"], side, side, 2), ("grp", "x", "y", "core")
    )
    seq = ("x", "y", "core")
    every = ("grp",) + seq
    in_specs = (
        P("grp", seq),
        P("grp", None),
        P("grp", seq, None),
        P("grp", seq, None),
        P(every, None, None),
        P(every, None, None),
        P(every),
        P(seq, None),
    )
    return jax.shard_map(
        body, mesh=fine, in_specs=in_specs, out_specs=P("grp", seq), check_vma=False
    )
```

```python
import math

import jax
import jax.numpy as jnp
from jax import lax
from jax.experimental import pallas as pl
from jax.experimental.pallas import tpu as pltpu
from jax.sharding import Mesh, PartitionSpec as P

QUERY_HEADS = 32
KEY_VALUE_HEADS = 4
HEAD_SIZE = 128
SUFFIX_SLOTS = 128
CAP = 8
PLANE = ("x", "y")
SWAP = ((0, 1), (1, 0))
TAIL = 16
FACTOR = 1.0 / math.sqrt(HEAD_SIZE)
LOG2E = 1.0 / math.log(2.0)
BIG = 28 * 1024 * 1024
MOST = 58 * 1024 * 1024
F32, BF16 = jnp.float32, jnp.bfloat16


def iota(shape, dim):
    return lax.broadcasted_iota(jnp.int32, shape, dim)


def matmul(a, b, ca=1, cb=0):
    return lax.dot_general(a, b, (((ca,), (cb,)), ((), ())), preferred_element_type=F32)


def high_part(value):
    return value.astype(BF16).astype(F32)


def whole_spec(shape):
    return pl.BlockSpec(shape, lambda *_: (0,) * len(shape))


HBM = pl.BlockSpec(memory_space=pltpu.HBM)
SMEM = pl.BlockSpec(memory_space=pltpu.SMEM)
VMEM = pl.BlockSpec(memory_space=pltpu.VMEM)
PIECES = 4


def layout_of(length, chips, feats, wide, suffix_rows):
    weights = 2 * length
    skeys = weights + chips * feats // 2
    svalues = skeys + suffix_rows
    lengths = svalues + suffix_rows
    return 0, length, weights, skeys, svalues, lengths, lengths + TAIL


def pack_kernel(prompt_ref, query_ref, packed_ref, place_ref, tails_ref):
    prompt = prompt_ref[...]
    slots, rows = place_ref.shape
    chips = tails_ref.shape[0] // TAIL
    lines = iota((slots, rows), 0)
    named = (lines == prompt).astype(F32)
    earlier = (iota((rows, rows), 0) < iota((rows, rows), 1)).astype(F32)
    before = matmul(named.astype(BF16), earlier.astype(BF16))
    rank = jnp.sum(before * named, axis=0, keepdims=True).astype(jnp.int32)
    place = (lines == prompt * CAP + rank).astype(F32).astype(BF16)
    place_ref[...] = place
    query = query_ref[...]
    packed_ref[...] = matmul(place, query).astype(BF16)

    line, row = iota((chips * TAIL, rows), 0), iota((chips * TAIL, rows), 1)
    spot = line & 7
    asks = (spot < 4) & (row == (line >> 4) * 4 + spot)
    tails_ref[...] = matmul(asks.astype(F32).astype(BF16), query).astype(BF16)


def pack(prompt, queries, slots, chips):
    rows = queries.shape[0]
    return pl.pallas_call(
        pack_kernel,
        out_shape=(
            jax.ShapeDtypeStruct((slots, HEAD_SIZE), BF16),
            jax.ShapeDtypeStruct((slots, rows), BF16),
            jax.ShapeDtypeStruct((chips * TAIL, HEAD_SIZE), BF16),
        ),
        compiler_params=pltpu.CompilerParams(vmem_limit_bytes=BIG),
        name="pack",
    )(prompt, queries)


def bundle_kernel(
    core_ref,
    len_ref,
    k_ref,
    v_ref,
    sk_ref,
    sv_ref,
    w_ref,
    bundle_ref,
    stage_ref,
    in_sems,
    out_sems,
):
    length, wide = k_ref.shape
    feats = w_ref.shape[0]
    chips = w_ref.shape[1] // wide
    width = wide // 2
    spots = layout_of(length, chips, feats, wide, sk_ref.shape[0])
    moves = []

    def move(source, rows, columns):
        copy = pltpu.make_async_copy(
            source, stage_ref.at[rows, columns], in_sems.at[len(moves)]
        )
        copy.start()
        moves.append((copy, rows, columns))

    piece = length // PIECES
    every = pl.ds(0, wide)
    for ref, first in ((k_ref, spots[0]), (v_ref, spots[1])):
        for i in range(PIECES):
            move(ref.at[pl.ds(i * piece, piece), :], pl.ds(first + i * piece, piece), every)
    other = 1 - core_ref[0]
    for k in range(chips):
        columns = pl.ds(pl.multiple_of(2 * width * k + other * width, width), width)
        rows = pl.ds(spots[2] + (k // 2) * feats, feats)
        move(w_ref.at[:, columns], rows, pl.ds((k % 2) * width, width))
    for ref, first in ((sk_ref, spots[3]), (sv_ref, spots[4])):
        move(ref, pl.ds(first, ref.shape[0]), every)
    line = iota((TAIL, wide), 0)
    lengths = jnp.where(line == 0, len_ref[0], jnp.where(line == 1, len_ref[1], 0))
    stage_ref[spots[5] :, :] = lengths.astype(F32).astype(BF16)

    leaving = []

    def leave(rows, columns):
        copy = pltpu.make_async_copy(
            stage_ref.at[rows, columns], bundle_ref.at[rows, columns], out_sems.at[len(leaving)]
        )
        copy.start()
        leaving.append(copy)

    leave(pl.ds(spots[5], TAIL), every)
    for copy, rows, columns in moves:
        copy.wait()
        leave(rows, columns)
    for copy in leaving:
        copy.wait()


def bundled(core, lengths, keys, values, skeys, svalues, w):
    length, wide = keys.shape
    chips = w.shape[1] // wide
    height = layout_of(length, chips, w.shape[0], wide, skeys.shape[0])[-1]
    return pl.pallas_call(
        bundle_kernel,
        in_specs=[SMEM, SMEM] + [HBM] * 5,
        out_specs=HBM,
        out_shape=jax.ShapeDtypeStruct((height, wide), BF16),
        scratch_shapes=[
            pltpu.VMEM((height, wide), BF16),
            pltpu.SemaphoreType.DMA((2 * PIECES + chips + 2,)),
            pltpu.SemaphoreType.DMA((2 * PIECES + chips + 3,)),
        ],
        compiler_params=pltpu.CompilerParams(vmem_limit_bytes=MOST),
        name="bundle",
    )(core, lengths, keys, values, skeys, svalues, w)


def asks_kernel(here_ref, asks_ref):
    asks_ref[...] = here_ref[...]


def asks_of(here):
    chips, height, _ = here.shape
    return pl.pallas_call(
        asks_kernel,
        grid=(1,),
        in_specs=[
            pl.BlockSpec((chips, TAIL, HEAD_SIZE), lambda i: (0, height // TAIL - 1, 0))
        ],
        out_specs=whole_spec((chips, TAIL, HEAD_SIZE)),
        out_shape=jax.ShapeDtypeStruct((chips, TAIL, HEAD_SIZE), BF16),
        cost_estimate=pl.CostEstimate(
            flops=20_000_000_000, bytes_accessed=1 << 20, transcendentals=0
        ),
        name="asks",
    )(here)


def spread_kernel(arrived_ref, tails_ref, out_ref):
    chips, height, _ = out_ref.shape
    arrived = arrived_ref[...]
    for k in range(chips):
        out_ref[k, : height - TAIL, :] = arrived
        out_ref[k, height - TAIL :, :] = tails_ref[k * TAIL : (k + 1) * TAIL]


def spread(arrived, tails, chips):
    return pl.pallas_call(
        spread_kernel,
        out_shape=jax.ShapeDtypeStruct((chips, arrived.shape[0] + TAIL, HEAD_SIZE), BF16),
        compiler_params=pltpu.CompilerParams(vmem_limit_bytes=BIG),
        name="spread",
    )(arrived, tails)


def suffix_part(core, lengths, query, keys, values):
    rows, span = query.shape[0], keys.shape[0]
    scores = matmul(query, keys, 1, 1)
    column = iota((rows, span), 1)
    block, place = column >> 7, column & 127
    live = ((iota((rows, span), 0) & 7) == ((block + 2 * core) & 3)) & (place < lengths)
    peak = jnp.max(jnp.where(live, scores, -1e30), axis=1, keepdims=True)
    shift = high_part(peak * FACTOR)
    weights = jnp.where(live, jnp.exp2(scores * (FACTOR * LOG2E) - shift * LOG2E), 0.0)
    ones = jnp.ones((span, HEAD_SIZE), BF16)
    outs = matmul(weights.astype(BF16), jnp.concatenate([values, ones], axis=1))
    lane = iota((rows, HEAD_SIZE), 1)
    total = outs[:, HEAD_SIZE:]
    total_high = high_part(total)
    numbers = jnp.where(
        lane == 0,
        shift,
        jnp.where(lane == 1, total_high, jnp.where(lane == 2, total - total_high, 0.0)),
    )
    line = iota((rows, HEAD_SIZE), 0) & (TAIL - 1)
    return jnp.where(
        line < 4, outs[:, :HEAD_SIZE], jnp.where((line >= 8) & (line < 12), numbers, 0.0)
    )


def attend_kernel(
    core_ref,
    len_ref,
    here_ref,
    asks_ref,
    k0_ref,
    k1_ref,
    v0_ref,
    v1_ref,
    sk0_ref,
    sk1_ref,
    sv0_ref,
    sv1_ref,
    other_len_ref,
    bundle_ref,
    out_ref,
    w_ref,
    even_ref,
    odd_ref,
    sems,
):
    step, steps = pl.program_id(0), pl.num_programs(0)
    total_heads = here_ref.shape[0]
    slots = here_ref.shape[1] - TAIL
    length, part = k0_ref.shape
    kv_heads = part // HEAD_SIZE
    heads = total_heads // kv_heads
    w_copy = pltpu.make_async_copy(
        bundle_ref.at[pl.ds(2 * length, w_ref.shape[0]), :], w_ref, sems.at[0]
    )

    @pl.when(step == 0)
    def _():
        w_copy.start()

    cuts = [slice(j * HEAD_SIZE, (j + 1) * HEAD_SIZE) for j in range(kv_heads)]
    ones = jnp.ones((length, HEAD_SIZE), BF16)
    held = (even_ref, odd_ref)
    units = [(j, j * heads + 2 * p) for j in range(kv_heads) for p in range(heads // 2)]

    def scores(unit):
        j, first = units[unit]
        query = jnp.concatenate([here_ref[first + i, :slots, :] for i in range(2)], axis=0)
        near = matmul(query, k0_ref[:, cuts[j]], 1, 1)
        held[unit % 2][:, :length] = near
        far = matmul(query, k1_ref[:, cuts[j]], 1, 1)
        held[unit % 2][:, length:] = far
        return jnp.max(jnp.maximum(near, far), axis=1, keepdims=True)

    peak = scores(0)
    others = other_len_ref[...].astype(F32)
    pick = lambda row: others[row : row + 1, :HEAD_SIZE].astype(jnp.int32)
    fixed = lambda row: jnp.full((1, HEAD_SIZE), len_ref[row], jnp.int32)
    lengths = jnp.concatenate([fixed(0), fixed(1), pick(0), pick(1)], axis=1)
    tails = []
    for j in range(kv_heads):
        asks = jnp.concatenate([asks_ref[j * heads + h] for h in range(heads)], axis=0)
        both = lambda a, b: jnp.concatenate([a[:, cuts[j]], b[:, cuts[j]]], axis=0)
        tails.append(
            suffix_part(core_ref[0], lengths, asks, both(sk0_ref, sk1_ref), both(sv0_ref, sv1_ref))
        )

    lane = iota((2 * slots, HEAD_SIZE), 1)
    for unit, (j, start) in enumerate(units):
        peak_next = scores(unit + 1) if unit + 1 < len(units) else None
        shift = high_part(peak * FACTOR)
        weights = jnp.exp2(held[unit % 2][...] * (FACTOR * LOG2E) - shift * LOG2E).astype(BF16)
        outs = matmul(weights[:, :length], jnp.concatenate([v0_ref[:, cuts[j]], ones], axis=1))
        outs += matmul(weights[:, length:], jnp.concatenate([v1_ref[:, cuts[j]], ones], axis=1))
        total = outs[:, HEAD_SIZE:]
        total_high = high_part(total)
        numbers = jnp.where(
            lane == 4,
            shift,
            jnp.where(lane == 5, total_high, jnp.where(lane == 6, total - total_high, 0.0)),
        )
        for i in range(2):
            h = start + i
            cut = slice(i * slots, (i + 1) * slots)
            out_ref[h, :slots, :] = outs[cut, :HEAD_SIZE].astype(BF16)
            place = (h - j * heads) * TAIL
            tail = tails[j][place : place + TAIL] + numbers[cut].T[:TAIL]
            out_ref[h, slots:, :] = tail.astype(BF16)
        peak = peak_next

    @pl.when(step == steps - 1)
    def _():
        w_copy.wait()


def attend(core, lengths, here, asks, keys, values, skeys, svalues, bundle):
    chips, height, _ = here.shape
    steps = 2
    heads = chips // steps
    length, wide = keys.shape
    part = wide // steps
    slots, own_suffix = height - TAIL, skeys.shape[0]
    spots = layout_of(length, chips, HEAD_SIZE, wide, own_suffix)
    chunk = pl.BlockSpec((heads, height, HEAD_SIZE), lambda j: (j, 0, 0))
    tail = pl.BlockSpec((heads, TAIL, HEAD_SIZE), lambda j: (j, 0, 0))
    block = lambda rows, first: pl.BlockSpec((rows, part), lambda j: (first // rows, j))
    w_rows = chips * HEAD_SIZE // 2
    return pl.pallas_call(
        attend_kernel,
        grid=(steps,),
        in_specs=[
            SMEM,
            SMEM,
            chunk,
            tail,
            block(length, 0),
            block(length, spots[0]),
            block(length, 0),
            block(length, spots[1]),
            block(own_suffix, 0),
            block(own_suffix, spots[3]),
            block(own_suffix, 0),
            block(own_suffix, spots[4]),
            pl.BlockSpec((TAIL, HEAD_SIZE), lambda j: (spots[5] // TAIL, 0)),
            HBM,
        ],
        out_specs=(chunk, whole_spec((w_rows, wide))),
        out_shape=(
            jax.ShapeDtypeStruct(here.shape, BF16),
            jax.ShapeDtypeStruct((w_rows, wide), BF16),
        ),
        scratch_shapes=[
            pltpu.VMEM((2 * slots, 2 * length), F32),
            pltpu.VMEM((2 * slots, 2 * length), F32),
            pltpu.SemaphoreType.DMA((1,)),
        ],
        compiler_params=pltpu.CompilerParams(vmem_limit_bytes=36 * 1024 * 1024),
        cost_estimate=pl.CostEstimate(
            flops=8 * chips * height * length * HEAD_SIZE,
            bytes_accessed=10 * length * wide,
            transcendentals=2 * chips * height * length,
        ),
        name="attend",
    )(
        core,
        lengths,
        here,
        asks,
        keys,
        bundle,
        values,
        bundle,
        skeys,
        bundle,
        svalues,
        bundle,
        bundle,
        bundle,
    )


def merge_kernel(own_ref, sent_ref):
    chips, height, _ = own_ref.shape
    slots, groups = height - TAIL, sent_ref.shape[0]
    tails = own_ref[:, slots:, :].astype(F32)
    shift = tails[:, 4, :]
    total = tails[:, 5, :] + tails[:, 6, :]
    top = jnp.max(shift, axis=0, keepdims=True)
    scale = jnp.exp(shift - top)
    whole = jnp.sum(total * scale, axis=0, keepdims=True)
    whole_high = high_part(whole)
    line = iota((8, slots), 0)
    numbers = jnp.where(
        line == 0, top, jnp.where(line == 1, whole_high, jnp.where(line == 2, whole - whole_high, 0.0))
    )
    rest = jnp.zeros((HEAD_SIZE - chips - 8, slots), F32)
    across = jnp.concatenate([scale / whole, numbers, rest], axis=0).T
    mean = jnp.zeros((slots, HEAD_SIZE), F32)
    for k in range(chips):
        mean += across[:, k : k + 1] * own_ref[k, :slots, :].astype(F32)
    cap = slots // groups
    both = [value.reshape(groups, cap, HEAD_SIZE) for value in (mean, across)]
    sent_ref[...] = jnp.concatenate(both, axis=1).astype(BF16)


def merge(own, groups):
    chips, height, _ = own.shape
    cap = (height - TAIL) // groups
    return pl.pallas_call(
        merge_kernel,
        out_shape=jax.ShapeDtypeStruct((groups, 2 * cap, HEAD_SIZE), BF16),
        compiler_params=pltpu.CompilerParams(vmem_limit_bytes=BIG),
        name="merge",
    )(own)


def finish_kernel(place_ref, back_ref, tails_ref, out_ref):
    groups, double, _ = back_ref.shape
    cap, rows = double // 2, place_ref.shape[1]
    chips = tails_ref.shape[0]
    span = chips * TAIL
    back = back_ref[...].astype(F32)
    means = back[:, :cap].reshape(groups * cap, HEAD_SIZE).astype(BF16)
    numbers = back[:, cap:].reshape(groups * cap, HEAD_SIZE).astype(BF16)
    both = matmul(place_ref[...], jnp.concatenate([means, numbers], axis=1), 0, 0)
    pre_mean, pre_numbers = both[:, :HEAD_SIZE], both[:, HEAD_SIZE:]
    pre_top = pre_numbers[:, chips : chips + 1]
    pre_total = pre_numbers[:, chips + 1 : chips + 2] + pre_numbers[:, chips + 2 : chips + 3]

    tails = tails_ref[...].reshape(span, HEAD_SIZE)
    line, column = iota((2 * rows, span), 0), iota((2 * rows, span), 1)
    row = line & (rows - 1)
    spot = (row >> 2) * TAIL + (row & 3) + jnp.where(line < rows, 0, 8)
    picked = matmul((column == spot).astype(F32).astype(BF16), tails)
    suf_out, suf_numbers = picked[:rows], picked[rows:]
    suf_top = suf_numbers[:, 0:1]
    suf_total = suf_numbers[:, 1:2] + suf_numbers[:, 2:3]

    peak = jnp.maximum(pre_top, suf_top)
    left = jnp.exp(pre_top - peak) * pre_total
    right = jnp.exp(suf_top - peak)
    attended = (pre_mean * left + suf_out * right) / (left + suf_total * right)
    out_ref[...] = attended.astype(BF16)


def finish(place, back, own):
    chips, height, _ = own.shape
    rows = place.shape[1]
    return pl.pallas_call(
        finish_kernel,
        grid=(1,),
        in_specs=[
            whole_spec(place.shape),
            whole_spec(back.shape),
            pl.BlockSpec((chips, TAIL, HEAD_SIZE), lambda i: (0, height // TAIL - 1, 0)),
        ],
        out_specs=whole_spec((rows, HEAD_SIZE)),
        out_shape=jax.ShapeDtypeStruct((rows, HEAD_SIZE), BF16),
        name="finish",
    )(place, back, own)


def project_kernel(core_ref, a_ref, w0_ref, w1_ref, out_ref):
    width = out_ref.shape[2]
    feats = w0_ref.shape[0]
    core = core_ref[0]
    attended = jnp.concatenate([a_ref[core], a_ref[1 - core]], axis=1)
    for k in range(out_ref.shape[0]):
        own = w0_ref[:, pl.ds(pl.multiple_of(2 * width * k + core * width, width), width)]
        half, side = (k // 2) * feats, (k % 2) * width
        other = w1_ref[half : half + feats, side : side + width]
        out_ref[k] = matmul(attended, jnp.concatenate([own, other], axis=0)).astype(BF16)


def project(core, attended, w, w_other, chips):
    _, rows, feats = attended.shape
    width = w.shape[1] // (2 * chips)
    steps = 2
    part = chips // steps
    high = part * feats // 2
    return pl.pallas_call(
        project_kernel,
        grid=(steps,),
        in_specs=[
            SMEM,
            whole_spec(attended.shape),
            pl.BlockSpec((feats, 2 * width * part), lambda i: (0, i)),
            pl.BlockSpec((high, 2 * width), lambda i: (i, 0)),
        ],
        out_specs=pl.BlockSpec((part, rows, width), lambda i: (i, 0, 0)),
        out_shape=jax.ShapeDtypeStruct((chips, rows, width), BF16),
        compiler_params=pltpu.CompilerParams(vmem_limit_bytes=BIG),
        name="project",
    )(core, attended, w, w_other)


def body(
    queries,
    row_prompt,
    prompt_prefix_keys,
    prompt_prefix_values,
    row_suffix_keys,
    row_suffix_values,
    suffix_lengths,
    w_out,
):
    groups = lax.axis_size("grp")
    chips = lax.axis_size("x") * lax.axis_size("y")
    core = lax.axis_index("core").reshape(1).astype(jnp.int32)
    row_grp = queries.shape[0]
    slots = groups * CAP
    keys, values = prompt_prefix_keys[0], prompt_prefix_values[0]
    skeys = row_suffix_keys.reshape(-1, row_suffix_keys.shape[2])
    svalues = row_suffix_values.reshape(-1, row_suffix_values.shape[2])

    packed, place, tails = pack(row_prompt.reshape(1, row_grp), queries, slots, chips)
    arrived = lax.all_to_all(packed, "grp", split_axis=0, concat_axis=0, tiled=True)

    _, late_lengths = lax.optimization_barrier((arrived, suffix_lengths))
    bundle = bundled(core, late_lengths, keys, values, skeys, svalues, w_out)
    bundle = lax.ppermute(bundle, "core", SWAP)
    here = lax.all_to_all(
        spread(arrived, tails, chips), PLANE, split_axis=0, concat_axis=0, tiled=True
    )
    parts, w_other = attend(
        core, suffix_lengths, here, asks_of(here), keys, values, skeys, svalues, bundle
    )
    own = lax.all_to_all(parts, PLANE, split_axis=0, concat_axis=0, tiled=True)

    sent = merge(own, groups)
    back = lax.all_to_all(sent, "grp", split_axis=0, concat_axis=0, tiled=True)
    attended = lax.all_gather(finish(place, back, own), "core", axis=0, tiled=False)
    shares = project(core, attended, w_out, w_other, chips)
    shares = lax.all_to_all(shares, PLANE, split_axis=0, concat_axis=0, tiled=True)
    return jnp.sum(shares.astype(F32), axis=0).astype(BF16)


def solution(mesh):
    side = math.isqrt(mesh.shape["seq"] // 2)
    fine = Mesh(
        mesh.devices.reshape(mesh.shape["grp"], side, side, 2), ("grp", "x", "y", "core")
    )
    seq = ("x", "y", "core")
    every = ("grp",) + seq
    in_specs = (
        P("grp", seq),
        P("grp", None),
        P("grp", seq, None),
        P("grp", seq, None),
        P(every, None, None),
        P(every, None, None),
        P(every),
        P(seq, None),
    )
    return jax.shard_map(
        body, mesh=fine, in_specs=in_specs, out_specs=P("grp", seq), check_vma=False
    )
```

```python
import math

import jax
import jax.numpy as jnp
from jax import lax
from jax.experimental import pallas as pl
from jax.experimental.pallas import tpu as pltpu
from jax.sharding import Mesh, PartitionSpec as P

QUERY_HEADS = 32
KEY_VALUE_HEADS = 4
HEAD_SIZE = 128
SUFFIX_SLOTS = 128
CAP = 8
PLANE = ("x", "y")
SWAP = ((0, 1), (1, 0))
TAIL = 16
FACTOR = 1.0 / math.sqrt(HEAD_SIZE)
LOG2E = 1.0 / math.log(2.0)
BIG = 28 * 1024 * 1024
MOST = 58 * 1024 * 1024
ROOMY = 24 * 1024
F32, BF16 = jnp.float32, jnp.bfloat16


def iota(shape, dim):
    return lax.broadcasted_iota(jnp.int32, shape, dim)


def matmul(a, b, ca=1, cb=0):
    return lax.dot_general(a, b, (((ca,), (cb,)), ((), ())), preferred_element_type=F32)


def high_part(value):
    return value.astype(BF16).astype(F32)


def whole_spec(shape):
    return pl.BlockSpec(shape, lambda *_: (0,) * len(shape))


HBM = pl.BlockSpec(memory_space=pltpu.HBM)
SMEM = pl.BlockSpec(memory_space=pltpu.SMEM)
VMEM = pl.BlockSpec(memory_space=pltpu.VMEM)
PIECES = 4


def layout_of(length, chips, feats, wide, suffix_rows):
    weights = 2 * length
    skeys = weights + chips * feats // 2
    svalues = skeys + suffix_rows
    lengths = svalues + suffix_rows
    return 0, length, weights, skeys, svalues, lengths, lengths + TAIL


def pack_kernel(
    core_ref,
    len_ref,
    prompt_ref,
    query_ref,
    k_ref,
    v_ref,
    sk_ref,
    sv_ref,
    w_ref,
    packed_ref,
    place_ref,
    tails_ref,
    bundle_ref,
    stage_ref,
    in_sems,
    out_sems,
):
    length, wide = k_ref.shape
    feats, chips = w_ref.shape[0], tails_ref.shape[0] // TAIL
    width = w_ref.shape[1] // (2 * chips)
    spots = layout_of(length, chips, feats, wide, sk_ref.shape[0])
    moves = []

    def move(source, rows, columns):
        copy = pltpu.make_async_copy(
            source, stage_ref.at[rows, columns], in_sems.at[len(moves)]
        )
        copy.start()
        moves.append((copy, rows, columns))

    piece = length // PIECES
    every = pl.ds(0, wide)
    for ref, first in ((k_ref, spots[0]), (v_ref, spots[1])):
        for i in range(PIECES):
            move(ref.at[pl.ds(i * piece, piece), :], pl.ds(first + i * piece, piece), every)
    other = 1 - core_ref[0]
    for k in range(chips):
        columns = pl.ds(pl.multiple_of(2 * width * k + other * width, width), width)
        rows = pl.ds(spots[2] + (k // 2) * feats, feats)
        move(w_ref.at[:, columns], rows, pl.ds((k % 2) * width, width))
    for ref, first in ((sk_ref, spots[3]), (sv_ref, spots[4])):
        move(ref, pl.ds(first, ref.shape[0]), every)
    line = iota((TAIL, wide), 0)
    lengths = jnp.where(line == 0, len_ref[0], jnp.where(line == 1, len_ref[1], 0))
    stage_ref[spots[5] :, :] = lengths.astype(F32).astype(BF16)

    prompt = prompt_ref[...]
    slots, rows = place_ref.shape
    lines = iota((slots, rows), 0)
    named = (lines == prompt).astype(F32)
    earlier = (iota((rows, rows), 0) < iota((rows, rows), 1)).astype(F32)
    before = matmul(named.astype(BF16), earlier.astype(BF16))
    rank = jnp.sum(before * named, axis=0, keepdims=True).astype(jnp.int32)
    place = (lines == prompt * CAP + rank).astype(F32).astype(BF16)
    place_ref[...] = place
    query = query_ref[...]
    packed_ref[...] = matmul(place, query).astype(BF16)

    line, row = iota((chips * TAIL, rows), 0), iota((chips * TAIL, rows), 1)
    spot = line & 7
    asks = (spot < 4) & (row == (line >> 4) * 4 + spot)
    tails_ref[...] = matmul(asks.astype(F32).astype(BF16), query).astype(BF16)

    leaving = []

    def leave(rows, columns):
        copy = pltpu.make_async_copy(
            stage_ref.at[rows, columns], bundle_ref.at[rows, columns], out_sems.at[len(leaving)]
        )
        copy.start()
        leaving.append(copy)

    leave(pl.ds(spots[5], TAIL), every)
    for copy, rows, columns in moves:
        copy.wait()
        leave(rows, columns)
    for copy in leaving:
        copy.wait()


def pack(core, lengths, prompt, queries, keys, values, skeys, svalues, w, slots, chips):
    rows = queries.shape[0]
    length, wide = keys.shape
    height = layout_of(length, chips, w.shape[0], wide, skeys.shape[0])[-1]
    return pl.pallas_call(
        pack_kernel,
        in_specs=[SMEM, SMEM, VMEM, VMEM] + [HBM] * 5,
        out_specs=(VMEM, VMEM, VMEM, HBM),
        out_shape=(
            jax.ShapeDtypeStruct((slots, HEAD_SIZE), BF16),
            jax.ShapeDtypeStruct((slots, rows), BF16),
            jax.ShapeDtypeStruct((chips * TAIL, HEAD_SIZE), BF16),
            jax.ShapeDtypeStruct((height, wide), BF16),
        ),
        scratch_shapes=[
            pltpu.VMEM((height, wide), BF16),
            pltpu.SemaphoreType.DMA((2 * PIECES + chips + 2,)),
            pltpu.SemaphoreType.DMA((2 * PIECES + chips + 3,)),
        ],
        compiler_params=pltpu.CompilerParams(vmem_limit_bytes=MOST),
        name="pack",
    )(core, lengths, prompt, queries, keys, values, skeys, svalues, w)


def spread_kernel(arrived_ref, tails_ref, out_ref):
    chips, height, _ = out_ref.shape
    arrived = arrived_ref[...]
    for k in range(chips):
        out_ref[k, : height - TAIL, :] = arrived
        out_ref[k, height - TAIL :, :] = tails_ref[k * TAIL : (k + 1) * TAIL]


def spread(arrived, tails, chips):
    return pl.pallas_call(
        spread_kernel,
        out_shape=jax.ShapeDtypeStruct((chips, arrived.shape[0] + TAIL, HEAD_SIZE), BF16),
        compiler_params=pltpu.CompilerParams(vmem_limit_bytes=BIG),
        name="spread",
    )(arrived, tails)


def suffix_part(core, lengths, query, keys, values):
    rows, span = query.shape[0], keys.shape[0]
    scores = matmul(query, keys, 1, 1)
    column = iota((rows, span), 1)
    block, place = column >> 7, column & 127
    live = ((iota((rows, span), 0) & 7) == ((block + 2 * core) & 3)) & (place < lengths)
    peak = jnp.max(jnp.where(live, scores, -1e30), axis=1, keepdims=True)
    shift = high_part(peak * FACTOR)
    weights = jnp.where(live, jnp.exp2(scores * (FACTOR * LOG2E) - shift * LOG2E), 0.0)
    ones = jnp.ones((span, HEAD_SIZE), BF16)
    outs = matmul(weights.astype(BF16), jnp.concatenate([values, ones], axis=1))
    lane = iota((rows, HEAD_SIZE), 1)
    total = outs[:, HEAD_SIZE:]
    total_high = high_part(total)
    numbers = jnp.where(
        lane == 0,
        shift,
        jnp.where(lane == 1, total_high, jnp.where(lane == 2, total - total_high, 0.0)),
    )
    line = iota((rows, HEAD_SIZE), 0) & (TAIL - 1)
    return jnp.where(
        line < 4, outs[:, :HEAD_SIZE], jnp.where((line >= 8) & (line < 12), numbers, 0.0)
    )


def attend_kernel(
    core_ref,
    len_ref,
    here_ref,
    k_ref,
    v_ref,
    sk_ref,
    sv_ref,
    bundle_ref,
    out_ref,
    w_ref,
    w_buf,
    k_buf,
    v_buf,
    sk_buf,
    sv_buf,
    len_buf,
    even_ref,
    odd_ref,
    sems,
):
    step = pl.program_id(0)
    steps = k_buf.shape[0]
    total_heads = here_ref.shape[0]
    slots = here_ref.shape[1] - TAIL
    length, wide = k_ref.shape
    chips = total_heads * steps
    own_suffix = sk_ref.shape[0]
    spots = layout_of(length, chips, HEAD_SIZE, wide, own_suffix)
    part = wide // steps
    kv_heads = part // HEAD_SIZE
    heads = total_heads // kv_heads
    parts = (
        (k_ref, spots[0], length, k_buf),
        (v_ref, spots[1], length, v_buf),
        (sk_ref, spots[3], own_suffix, sk_buf),
        (sv_ref, spots[4], own_suffix, sv_buf),
    )

    def copies(i, s):
        ref, first, count, buf = parts[i]
        columns = pl.ds(pl.multiple_of(s * part, part), part)
        return (
            pltpu.make_async_copy(
                ref.at[:, columns], buf.at[s, pl.ds(0, count)], sems.at[s, 2 * i]
            ),
            pltpu.make_async_copy(
                bundle_ref.at[pl.ds(first, count), columns],
                buf.at[s, pl.ds(count, count)],
                sems.at[s, 2 * i + 1],
            ),
        )

    len_copy = pltpu.make_async_copy(
        bundle_ref.at[pl.ds(spots[5], TAIL), :], len_buf, sems.at[0, 2 * len(parts)]
    )

    w_in = pltpu.make_async_copy(
        bundle_ref.at[pl.ds(spots[2], w_buf.shape[0]), :], w_buf, sems.at[1, 2 * len(parts)]
    )
    w_out = pltpu.make_async_copy(
        w_buf, w_ref.at[pl.ds(0, w_buf.shape[0]), :], sems.at[0, 2 * len(parts) + 1]
    )


    @pl.when(step == 0)
    def _():
        for s in range(steps):
            for i in (0, 2, 3, 1):
                for copy in copies(i, s):
                    copy.start()
            if s == 0:
                len_copy.start()
        w_in.start()
        len_copy.wait()

    @pl.when(step == steps - 1)
    def _():
        w_in.wait()
        w_out.start()

    def arrive(i):
        for copy in copies(i, step):
            copy.wait()

    cuts = [slice(j * HEAD_SIZE, (j + 1) * HEAD_SIZE) for j in range(kv_heads)]
    ones = jnp.ones((2 * length, HEAD_SIZE), BF16)
    held = (even_ref, odd_ref)
    units = [(j, j * heads + 2 * p) for j in range(kv_heads) for p in range(heads // 2)]

    def scores(unit):
        j, first = units[unit]
        query = jnp.concatenate([here_ref[first + i, :slots, :] for i in range(2)], axis=0)
        value = matmul(query, k_buf[step, :, cuts[j]], 1, 1)
        held[unit % 2][...] = value
        return jnp.max(value, axis=1, keepdims=True)

    arrive(0)
    peak = scores(0)
    arrive(2)
    arrive(3)
    span = 2 * own_suffix
    block = iota((1, span), 1) >> 7
    others = len_buf[...].astype(F32)
    pick = lambda row: others[row : row + 1, :HEAD_SIZE].astype(jnp.int32)
    fixed = lambda row: jnp.full((1, HEAD_SIZE), len_ref[row], jnp.int32)
    lengths = jnp.concatenate([fixed(0), fixed(1), pick(0), pick(1)], axis=1)
    tails = []
    for j in range(kv_heads):
        asks = jnp.concatenate([here_ref[j * heads + h, slots:, :] for h in range(heads)], axis=0)
        tails.append(
            suffix_part(
                core_ref[0], lengths, asks, sk_buf[step, :, cuts[j]], sv_buf[step, :, cuts[j]]
            )
        )
    arrive(1)

    lane = iota((2 * slots, HEAD_SIZE), 1)
    for unit, (j, start) in enumerate(units):
        peak_next = scores(unit + 1) if unit + 1 < len(units) else None
        shift = high_part(peak * FACTOR)
        weights = jnp.exp2(held[unit % 2][...] * (FACTOR * LOG2E) - shift * LOG2E).astype(BF16)
        outs = matmul(weights, jnp.concatenate([v_buf[step, :, cuts[j]], ones], axis=1))
        total = outs[:, HEAD_SIZE:]
        total_high = high_part(total)
        numbers = jnp.where(
            lane == 4,
            shift,
            jnp.where(lane == 5, total_high, jnp.where(lane == 6, total - total_high, 0.0)),
        )
        for i in range(2):
            h = start + i
            cut = slice(i * slots, (i + 1) * slots)
            out_ref[h, :slots, :] = outs[cut, :HEAD_SIZE].astype(BF16)
            place = (h - j * heads) * TAIL
            tail = tails[j][place : place + TAIL] + numbers[cut].T[:TAIL]
            out_ref[h, slots:, :] = tail.astype(BF16)
        peak = peak_next

    @pl.when(step == steps - 1)
    def _():
        w_out.wait()


def attend(core, lengths, here, keys, values, skeys, svalues, bundle):
    chips, height, _ = here.shape
    steps = 2
    heads = chips // steps
    length, wide = keys.shape
    part = wide // steps
    slots, own_suffix = height - TAIL, skeys.shape[0]
    chunk = pl.BlockSpec((heads, height, HEAD_SIZE), lambda j: (j, 0, 0))
    return pl.pallas_call(
        attend_kernel,
        grid=(steps,),
        in_specs=[SMEM, SMEM, chunk] + [HBM] * 5,
        out_specs=(chunk, HBM),
        out_shape=(
            jax.ShapeDtypeStruct(here.shape, BF16),
            jax.ShapeDtypeStruct((ROOMY, wide), BF16),
        ),
        scratch_shapes=[
            pltpu.VMEM((chips * HEAD_SIZE // 2, wide), BF16),
            pltpu.VMEM((steps, 2 * length, part), BF16),
            pltpu.VMEM((steps, 2 * length, part), BF16),
            pltpu.VMEM((steps, 2 * own_suffix, part), BF16),
            pltpu.VMEM((steps, 2 * own_suffix, part), BF16),
            pltpu.VMEM((TAIL, wide), BF16),
            pltpu.VMEM((2 * slots, 2 * length), F32),
            pltpu.VMEM((2 * slots, 2 * length), F32),
            pltpu.SemaphoreType.DMA((steps, 10)),
        ],
        compiler_params=pltpu.CompilerParams(vmem_limit_bytes=40 * 1024 * 1024),
        cost_estimate=pl.CostEstimate(
            flops=8 * chips * height * length * HEAD_SIZE,
            bytes_accessed=10 * length * wide,
            transcendentals=2 * chips * height * length,
        ),
        name="attend",
    )(core, lengths, here, keys, values, skeys, svalues, bundle)


def merge_kernel(own_ref, sent_ref):
    chips, height, _ = own_ref.shape
    slots, groups = height - TAIL, sent_ref.shape[0]
    tails = own_ref[:, slots:, :].astype(F32)
    shift = tails[:, 4, :]
    total = tails[:, 5, :] + tails[:, 6, :]
    top = jnp.max(shift, axis=0, keepdims=True)
    scale = jnp.exp(shift - top)
    whole = jnp.sum(total * scale, axis=0, keepdims=True)
    whole_high = high_part(whole)
    line = iota((8, slots), 0)
    numbers = jnp.where(
        line == 0, top, jnp.where(line == 1, whole_high, jnp.where(line == 2, whole - whole_high, 0.0))
    )
    rest = jnp.zeros((HEAD_SIZE - chips - 8, slots), F32)
    across = jnp.concatenate([scale / whole, numbers, rest], axis=0).T
    mean = jnp.zeros((slots, HEAD_SIZE), F32)
    for k in range(chips):
        mean += across[:, k : k + 1] * own_ref[k, :slots, :].astype(F32)
    cap = slots // groups
    both = [value.reshape(groups, cap, HEAD_SIZE) for value in (mean, across)]
    sent_ref[...] = jnp.concatenate(both, axis=1).astype(BF16)


def merge(own, groups):
    chips, height, _ = own.shape
    cap = (height - TAIL) // groups
    return pl.pallas_call(
        merge_kernel,
        out_shape=jax.ShapeDtypeStruct((groups, 2 * cap, HEAD_SIZE), BF16),
        compiler_params=pltpu.CompilerParams(vmem_limit_bytes=BIG),
        name="merge",
    )(own)


def finish_kernel(place_ref, back_ref, tails_ref, out_ref):
    groups, double, _ = back_ref.shape
    cap, rows = double // 2, place_ref.shape[1]
    chips = tails_ref.shape[0]
    span = chips * TAIL
    back = back_ref[...].astype(F32)
    means = back[:, :cap].reshape(groups * cap, HEAD_SIZE).astype(BF16)
    numbers = back[:, cap:].reshape(groups * cap, HEAD_SIZE).astype(BF16)
    both = matmul(place_ref[...], jnp.concatenate([means, numbers], axis=1), 0, 0)
    pre_mean, pre_numbers = both[:, :HEAD_SIZE], both[:, HEAD_SIZE:]
    pre_top = pre_numbers[:, chips : chips + 1]
    pre_total = pre_numbers[:, chips + 1 : chips + 2] + pre_numbers[:, chips + 2 : chips + 3]

    tails = tails_ref[...].reshape(span, HEAD_SIZE)
    line, column = iota((2 * rows, span), 0), iota((2 * rows, span), 1)
    row = line & (rows - 1)
    spot = (row >> 2) * TAIL + (row & 3) + jnp.where(line < rows, 0, 8)
    picked = matmul((column == spot).astype(F32).astype(BF16), tails)
    suf_out, suf_numbers = picked[:rows], picked[rows:]
    suf_top = suf_numbers[:, 0:1]
    suf_total = suf_numbers[:, 1:2] + suf_numbers[:, 2:3]

    peak = jnp.maximum(pre_top, suf_top)
    left = jnp.exp(pre_top - peak) * pre_total
    right = jnp.exp(suf_top - peak)
    attended = (pre_mean * left + suf_out * right) / (left + suf_total * right)
    out_ref[...] = attended.astype(BF16)


def finish(place, back, own):
    chips, height, _ = own.shape
    rows = place.shape[1]
    return pl.pallas_call(
        finish_kernel,
        grid=(1,),
        in_specs=[
            whole_spec(place.shape),
            whole_spec(back.shape),
            pl.BlockSpec((chips, TAIL, HEAD_SIZE), lambda i: (0, height // TAIL - 1, 0)),
        ],
        out_specs=whole_spec((rows, HEAD_SIZE)),
        out_shape=jax.ShapeDtypeStruct((rows, HEAD_SIZE), BF16),
        name="finish",
    )(place, back, own)


def project_kernel(core_ref, a_ref, w0_ref, w1_ref, out_ref):
    width = out_ref.shape[2]
    feats = w0_ref.shape[0]
    core = core_ref[0]
    attended = jnp.concatenate([a_ref[core], a_ref[1 - core]], axis=1)
    for k in range(out_ref.shape[0]):
        own = w0_ref[:, pl.ds(pl.multiple_of(2 * width * k + core * width, width), width)]
        half, side = (k // 2) * feats, (k % 2) * width
        other = w1_ref[half : half + feats, side : side + width]
        out_ref[k] = matmul(attended, jnp.concatenate([own, other], axis=0)).astype(BF16)


def project(core, attended, w, w_other, chips):
    _, rows, feats = attended.shape
    width = w.shape[1] // (2 * chips)
    steps = 2
    part = chips // steps
    high = part * feats // 2
    return pl.pallas_call(
        project_kernel,
        grid=(steps,),
        in_specs=[
            SMEM,
            whole_spec(attended.shape),
            pl.BlockSpec((feats, 2 * width * part), lambda i: (0, i)),
            pl.BlockSpec((high, 2 * width), lambda i: (i, 0)),
        ],
        out_specs=pl.BlockSpec((part, rows, width), lambda i: (i, 0, 0)),
        out_shape=jax.ShapeDtypeStruct((chips, rows, width), BF16),
        compiler_params=pltpu.CompilerParams(vmem_limit_bytes=BIG),
        name="project",
    )(core, attended, w, w_other)


def body(
    queries,
    row_prompt,
    prompt_prefix_keys,
    prompt_prefix_values,
    row_suffix_keys,
    row_suffix_values,
    suffix_lengths,
    w_out,
):
    groups = lax.axis_size("grp")
    chips = lax.axis_size("x") * lax.axis_size("y")
    core = lax.axis_index("core").reshape(1).astype(jnp.int32)
    row_grp = queries.shape[0]
    slots = groups * CAP
    keys, values = prompt_prefix_keys[0], prompt_prefix_values[0]
    skeys = row_suffix_keys.reshape(-1, row_suffix_keys.shape[2])
    svalues = row_suffix_values.reshape(-1, row_suffix_values.shape[2])

    packed, place, tails, bundle = pack(
        core,
        suffix_lengths,
        row_prompt.reshape(1, row_grp),
        queries,
        keys,
        values,
        skeys,
        svalues,
        w_out,
        slots,
        chips,
    )
    bundle = lax.ppermute(bundle, "core", SWAP)
    arrived = lax.all_to_all(packed, "grp", split_axis=0, concat_axis=0, tiled=True)

    here = lax.all_to_all(
        spread(arrived, tails, chips), PLANE, split_axis=0, concat_axis=0, tiled=True
    )
    parts, w_other = attend(core, suffix_lengths, here, keys, values, skeys, svalues, bundle)
    own = lax.all_to_all(parts, PLANE, split_axis=0, concat_axis=0, tiled=True)

    sent = merge(own, groups)
    back = lax.all_to_all(sent, "grp", split_axis=0, concat_axis=0, tiled=True)
    attended = lax.all_gather(finish(place, back, own), "core", axis=0, tiled=False)
    shares = project(core, attended, w_out, w_other, chips)
    shares = lax.all_to_all(shares, PLANE, split_axis=0, concat_axis=0, tiled=True)
    return jnp.sum(shares.astype(F32), axis=0).astype(BF16)


def solution(mesh):
    side = math.isqrt(mesh.shape["seq"] // 2)
    fine = Mesh(
        mesh.devices.reshape(mesh.shape["grp"], side, side, 2), ("grp", "x", "y", "core")
    )
    seq = ("x", "y", "core")
    every = ("grp",) + seq
    in_specs = (
        P("grp", seq),
        P("grp", None),
        P("grp", seq, None),
        P("grp", seq, None),
        P(every, None, None),
        P(every, None, None),
        P(every),
        P(seq, None),
    )
    return jax.shard_map(
        body, mesh=fine, in_specs=in_specs, out_specs=P("grp", seq), check_vma=False
    )
```
